32 devices in a mesh: groups: 2 (over x), slab: 16 (over z, y, core).
Axes of the slice: x: 2, y: 2, z: 4, core: 2. Of those that a mesh axis runs over, the one named last changes fastest.
Arguments:
- queries: bfloat16 [32, 8192], P(('groups', 'slab')), parts along dimension 0, may hold values from -40 to 40
- prefix_keys: bfloat16 [32768, 1024], P(('groups', 'slab')), parts along dimension 0, may hold values from -5 to 5
- prefix_values: bfloat16 [32768, 1024], P(('groups', 'slab')), parts along dimension 0, may hold values from -6 to 6
- block_ids: int32 [32, 32], P('groups'), parts along dimension 0, may hold values from 0 to 127, as said below
Outputs:
- attended: bfloat16 [32, 8192], P(('groups', 'slab')), parts along dimension 0
- log_totals: float32 [32, 64], P(('groups', 'slab')), parts along dimension 0
The draws below stay inside these ranges and needn't reach their ends.
There are 2 independent parts, one for each index of `groups`. The reference program is written for one: setup_inputs(seed, part) draws one part's arguments, and reference() takes and returns one part's arrays. A program takes and returns all parts, laid end to end along the dimension named above; each array names one. Nothing has to cross between parts.
Inputs may be any that keep to these rules, and one draw needn't show every extreme that they name: `block_ids`: each row names 32 different blocks of the 128 in rising order.
All inputs are finite; a program needn't handle non-finite values.
Results may differ from the reference program's by a relative error of at most 0.0065.
Values may be sent and summed in bfloat16 or wider, within the bound.
A program may use at most 64 MiB of HBM per device.

```python
import math
import jax
import jax.numpy as jnp
from jax import lax

H = 64
KVH = 8
HD = 128
BLOCK = 128
TOPK = 32
R_DEV = 1
BLOCKS_PER_SLAB = 8
CLASSES = 1
REQ = 16
NBLK = 128
PREFIX = 16384


def pick_blocks(key):
    root_key = jax.random.fold_in(key, 101)
    slab_score_total = NBLK // BLOCKS_PER_SLAB
    slab_extra_score = jax.random.randint(jax.random.fold_in(root_key, 1), (slab_score_total,), 0, 1024)
    noise_component = jax.random.randint(jax.random.fold_in(root_key, 2), (REQ, NBLK), 0, 4096)
    owner_keys = jax.random.split(jax.random.fold_in(root_key, 3), slab_score_total)
    orders = jax.vmap(lambda single: jax.random.permutation(single, slab_score_total))(owner_keys).astype(jnp.int32)
    request_line = jnp.arange(REQ, dtype=jnp.int32)
    owner_of = request_line // R_DEV
    class_of = request_line % R_DEV % CLASSES
    slab_value = jnp.take(orders, owner_of, axis=0)
    block_value = jnp.repeat(slab_value, BLOCKS_PER_SLAB, axis=1)
    allowed = block_value % CLASSES == class_of[:, None]
    block_line = jnp.arange(NBLK, dtype=jnp.int32)
    forced_choice = (block_value == class_of[:, None]) & (block_line % BLOCKS_PER_SLAB == 0)[None, :]
    raw_score = noise_component + jnp.repeat(slab_extra_score, BLOCKS_PER_SLAB)[None, :] + 8192 * forced_choice.astype(jnp.int32)
    scores = raw_score * NBLK + block_line[None, :]
    scores = jnp.where(allowed, scores, -1 - block_line[None, :])
    chosen = lax.top_k(scores, TOPK)[1]
    return jnp.sort(chosen, axis=1).astype(jnp.int32)


def drawn(key):
    root_key = jax.random.fold_in(key, 202)
    base_keys = jax.random.truncated_normal(jax.random.fold_in(root_key, 1), -5.0, 5.0, (PREFIX, KVH * HD), jnp.float32)
    query_base = 2.0 * jax.random.truncated_normal(jax.random.fold_in(root_key, 3), -6.0, 6.0, (REQ, H * HD), jnp.float32)
    return (base_keys, query_base)


def draw_block_ids(key, part):
    return pick_blocks(key)


def draw_prefix_keys(key, part):
    return drawn(key)[0].astype(jnp.bfloat16)


def draw_queries(key, part):
    return drawn(key)[1].astype(jnp.bfloat16)


def steps_of(stream_key, dims, cuts, least, top_value):
    level = 1.0
    for axis_at, shards_of in cuts:
        draws = jax.random.uniform(jax.random.fold_in(jax.random.fold_in(stream_key, 6), axis_at), (shards_of,), jnp.float32, least / len(cuts), top_value / len(cuts))
        level = level * jnp.repeat(jnp.exp(draws), dims[axis_at] // shards_of).reshape((-1,) + (1,) * (len(dims) - 1 - axis_at))
    return level


def scatter_about(own_key, dims, spread, bound, cuts=(), held_as=jnp.bfloat16):
    drawn = spread * jax.random.normal(own_key, dims, jnp.float32)
    if cuts:
        drawn = drawn * steps_of(own_key, dims, cuts, -0.22, 0.18)
    return jnp.clip(drawn, -bound, bound).astype(held_as)


def setup_inputs(seed: int = 0, part: int = 0) -> dict:
    arg_keys = jax.random.split(jax.random.key(seed), 5)
    part_keys = jax.random.split(jax.random.fold_in(arg_keys[4], part), 5)
    queries = draw_queries(jax.random.fold_in(jax.random.fold_in(arg_keys[4], part), 71), part)
    prefix_keys = draw_prefix_keys(jax.random.fold_in(jax.random.fold_in(arg_keys[4], part), 71), part)
    prefix_values = scatter_about(part_keys[2], (PREFIX, KVH * HD), 1.0, 6.0, ((0, 16),))
    block_ids = draw_block_ids(jax.random.fold_in(jax.random.fold_in(arg_keys[4], part), 71), part)
    return {"queries": queries, "prefix_keys": prefix_keys, "prefix_values": prefix_values, "block_ids": block_ids}


def reference(queries, prefix_keys, prefix_values, block_ids):
    key_blocks = prefix_keys.reshape(NBLK, BLOCK, KVH, HD)
    value_blocks = prefix_values.reshape(NBLK, BLOCK, KVH, HD)
    factor = 1.0 / math.sqrt(HD)

    def handle(request):
        query_row, chosen = request
        head_rows = query_row.reshape(KVH, H // KVH, HD).astype(jnp.float32)
        picked_keys = jnp.take(key_blocks, chosen.astype(jnp.int32), axis=0).reshape(TOPK * BLOCK, KVH, HD).astype(jnp.float32)
        picked_values = jnp.take(value_blocks, chosen.astype(jnp.int32), axis=0).reshape(TOPK * BLOCK, KVH, HD).astype(jnp.float32)
        scores = jnp.einsum('kgd,lkd->kgl', head_rows, picked_keys) * factor
        row_max = lax.optimization_barrier(jnp.max(scores, axis=-1, keepdims=True))
        weights = jnp.exp(scores - row_max)
        row_total = lax.optimization_barrier(jnp.sum(weights, axis=-1))
        rounded = weights.astype(jnp.bfloat16).astype(jnp.float32)
        mixed_sum = jnp.einsum('kgl,lkd->kgd', rounded, picked_values)
        attended_row = (mixed_sum / row_total[..., None]).astype(jnp.bfloat16).reshape(H * HD)
        log_row = (row_max[..., 0] + jnp.log(row_total)).reshape(H)
        return (attended_row, log_row)
    attended, log_totals = lax.map(handle, (queries, block_ids))
    return (attended, log_totals)
```

```python
import functools
import math

import jax
import jax.numpy as jnp
from jax import lax
from jax.experimental import pallas as pl
from jax.experimental.pallas import tpu as pltpu
from jax.sharding import PartitionSpec as P

HD = 128
BLOCK = 128
SUB = 8
TILE = 16
CHUNK = 16
MESH = pl.DeviceIdType.MESH

masked_score = -1e30


def kernel(
    n, q_hbm, k_hbm, v_hbm, ids_hbm, att_ref, log_ref,
    q_raw, q_own, ids, kbuf, vbuf, held, bias, out, out_stat, got, got_stat,
    load_sem, q_send, q_recv, o_send, o_recv, s_send, s_recv,
):
    me = lax.axis_index("slab")
    heads = q_own.shape[0]
    kv_heads = kbuf.shape[1] // HD
    pairs = heads // TILE
    span = kbuf.shape[0]
    blocks_here = span // BLOCK
    chunk = min(CHUNK, n)
    chunks = n // chunk
    factor = 1.0 / math.sqrt(HD)
    factor2 = factor * math.log2(math.e)

    barrier = pltpu.get_barrier_semaphore()

    def peer_of(i):
        return lax.rem(me + i, n)

    @pl.loop(1, n)
    def _(i):
        pl.semaphore_signal(barrier, inc=1, device_id={"slab": peer_of(i)}, device_id_type=MESH)

    loads = [
        pltpu.make_async_copy(src, dst, load_sem.at[at])
        for at, (src, dst) in enumerate(((q_hbm, q_raw), (ids_hbm, ids), (k_hbm, kbuf), (v_hbm, vbuf)))
    ]
    for load in loads:
        load.start()

    loads[0].wait()
    row = q_raw[...].astype(jnp.float32)
    q_own[...] = jnp.concatenate(
        [row[:, h * HD : (h + 1) * HD] for h in range(heads)], axis=0
    ).astype(jnp.bfloat16)

    pl.semaphore_wait(barrier, n - 1)

    @pl.loop(1, n)
    def _(i):
        pltpu.make_async_remote_copy(
            src_ref=q_own, dst_ref=held.at[me], send_sem=q_send, recv_sem=q_recv,
            device_id={"slab": peer_of(i)}, device_id_type=MESH,
        ).start()

    held[me] = q_own[...]

    loads[1].wait()

    def fill_bias(c):
        rows = pl.ds(c * chunk, chunk)
        wide = jnp.broadcast_to(ids[rows][:, None, :], (chunk, SUB, ids.shape[1]))
        for j in range(blocks_here):
            hit = jnp.where(wide == me * blocks_here + j, 0.0, masked_score)
            hit = jnp.max(hit, axis=-1, keepdims=True)
            bias[rows, :, j * BLOCK : (j + 1) * BLOCK] = jnp.broadcast_to(hit, (chunk, SUB, BLOCK))

    def each_chunk(body):
        if chunks == 1:
            body(0)
        else:
            pl.loop(0, chunks)(body)

    each_chunk(fill_bias)
    loads[2].wait()
    loads[3].wait()

    def whole(ref_at, send, recv):
        return pltpu.make_async_remote_copy(
            src_ref=ref_at, dst_ref=ref_at, send_sem=send, recv_sem=recv,
            device_id={"slab": peer_of(1)}, device_id_type=MESH,
        )

    others = pl.ds(0, n - 1)
    whole(held.at[others], q_send, q_recv).wait_recv()

    lane = lax.broadcasted_iota(jnp.int32, (chunk, SUB, HD), 2)
    sub = lax.broadcasted_iota(jnp.int32, (chunk * TILE, HD), 0)
    first = (lax.rem(sub, TILE) < SUB).astype(jnp.float32).astype(jnp.bfloat16)
    second = (lax.rem(sub, TILE) >= SUB).astype(jnp.float32).astype(jnp.bfloat16)

    for p in range(pairs):
        rows16 = slice(TILE * p, TILE * (p + 1))
        cols = slice(2 * HD * p, 2 * HD * (p + 1))

        def partial(c, p=p, rows16=rows16, cols=cols):
            rows = pl.ds(c * chunk, chunk)
            q = held[rows, rows16, :].reshape(chunk * TILE, HD)
            q = jnp.concatenate([q * first, q * second], axis=1)
            scores = lax.dot_general(
                q, kbuf[:, cols], (((1,), (1,)), ((), ())), preferred_element_type=jnp.float32
            ).reshape(chunk, 2, SUB, span)
            scores = scores + bias[rows][:, None]
            peak = jnp.max(scores, axis=-1, keepdims=True)
            weights = jnp.exp2((scores - peak) * factor2)
            total = jnp.sum(weights, axis=-1, keepdims=True)
            mixed = jnp.dot(
                weights.astype(jnp.bfloat16).reshape(chunk * TILE, span), vbuf[:, cols],
                preferred_element_type=jnp.float32,
            ).reshape(chunk, 2, SUB, 2 * HD)
            mixed = jnp.concatenate([mixed[:, 0:1, :, :HD], mixed[:, 1:2, :, HD:]], axis=1) / total
            out[rows, rows16, :] = mixed.reshape(chunk, TILE, HD).astype(jnp.bfloat16)
            logs = peak * factor + jnp.log(total)
            stat = jnp.zeros((chunk, SUB, HD), jnp.float32) if p == 0 else out_stat[rows]
            stat = jnp.where(lane == 2 * p, logs[:, 0], stat)
            out_stat[rows] = jnp.where(lane == 2 * p + 1, logs[:, 1], stat)

        each_chunk(partial)

        @pl.loop(1, n)
        def _(i, p=p, rows16=rows16):
            peer = peer_of(i)
            pltpu.make_async_remote_copy(
                src_ref=out.at[peer, rows16], dst_ref=got.at[me, rows16],
                send_sem=o_send.at[p], recv_sem=o_recv.at[p],
                device_id={"slab": peer}, device_id_type=MESH,
            ).start()

    @pl.loop(1, n)
    def _(i):
        peer = peer_of(i)
        pltpu.make_async_remote_copy(
            src_ref=out_stat.at[peer], dst_ref=got_stat.at[me], send_sem=s_send, recv_sem=s_recv,
            device_id={"slab": peer}, device_id_type=MESH,
        ).start()

    got[me] = out[me]
    got_stat[me] = out_stat[me]

    whole(got_stat.at[others], s_send, s_recv).wait_recv()
    logs = got_stat[...]
    peak = jnp.max(logs, axis=0)
    shares = jnp.exp(logs - peak[None])
    total = jnp.sum(shares, axis=0)
    shares = shares / total[None]
    joint = peak + jnp.log(total)

    head_lane = lax.broadcasted_iota(jnp.int32, (SUB, heads), 1)
    head_sub = lax.broadcasted_iota(jnp.int32, (SUB, heads), 0)
    spread = jnp.zeros((SUB, heads), jnp.float32)
    for k in range(kv_heads):
        spread = jnp.where(head_lane // SUB == k, joint[:, k : k + 1], spread)
    spread = jnp.where(lax.rem(head_lane, SUB) == head_sub, spread, 0.0)
    log_ref[...] = jnp.sum(spread, axis=0, keepdims=True)

    for p in range(pairs):
        rows16 = slice(TILE * p, TILE * (p + 1))
        whole(got.at[others, rows16], o_send.at[p], o_recv.at[p]).wait_recv()
        parts = got[:, rows16, :].astype(jnp.float32).reshape(n, 2, SUB, HD)
        merged = [
            jnp.sum(parts[:, half] * shares[:, :, 2 * p + half : 2 * p + half + 1], axis=0) for half in range(2)
        ]
        att_ref[rows16, :] = jnp.concatenate(merged, axis=0).astype(jnp.bfloat16)

    whole(held.at[others], q_send, q_recv).wait_send()
    whole(got_stat.at[others], s_send, s_recv).wait_send()
    for p in range(pairs):
        rows16 = slice(TILE * p, TILE * (p + 1))
        whole(got.at[others, rows16], o_send.at[p], o_recv.at[p]).wait_send()


def shards(queries, prefix_keys, prefix_values, block_ids):
    n = lax.axis_size("slab")
    rows, width = queries.shape
    span, kv_width = prefix_keys.shape
    heads = width // HD
    pairs = heads // TILE
    assert rows == 1 and block_ids.shape[0] == n and heads == SUB * (kv_width // HD)
    anywhere = pl.BlockSpec(memory_space=pltpu.HBM)
    in_vmem = pl.BlockSpec(memory_space=pltpu.VMEM)
    attended, log_totals = pl.pallas_call(
        functools.partial(kernel, n),
        out_shape=(
            jax.ShapeDtypeStruct((heads, HD), jnp.bfloat16),
            jax.ShapeDtypeStruct((1, heads), jnp.float32),
        ),
        in_specs=[anywhere] * 4,
        out_specs=(in_vmem, in_vmem),
        scratch_shapes=[
            pltpu.VMEM((1, width), jnp.bfloat16),
            pltpu.VMEM((heads, HD), jnp.bfloat16),
            pltpu.VMEM(block_ids.shape, jnp.int32),
            pltpu.VMEM((span, kv_width), jnp.bfloat16),
            pltpu.VMEM((span, kv_width), jnp.bfloat16),
            pltpu.VMEM((n, heads, HD), jnp.bfloat16),
            pltpu.VMEM((n, SUB, span), jnp.float32),
            pltpu.VMEM((n, heads, HD), jnp.bfloat16),
            pltpu.VMEM((n, SUB, HD), jnp.float32),
            pltpu.VMEM((n, heads, HD), jnp.bfloat16),
            pltpu.VMEM((n, SUB, HD), jnp.float32),
            pltpu.SemaphoreType.DMA((4,)),
            pltpu.SemaphoreType.DMA,
            pltpu.SemaphoreType.DMA,
            pltpu.SemaphoreType.DMA((pairs,)),
            pltpu.SemaphoreType.DMA((pairs,)),
            pltpu.SemaphoreType.DMA,
            pltpu.SemaphoreType.DMA,
        ],
        compiler_params=pltpu.CompilerParams(
            collective_id=0, has_side_effects=True, vmem_limit_bytes=48 * 1024 * 1024
        ),
        cost_estimate=pl.CostEstimate(
            flops=8 * n * heads * span * HD,
            bytes_accessed=4 * span * kv_width,
            transcendentals=n * heads * span,
        ),
    )(queries, prefix_keys, prefix_values, block_ids)
    return attended.reshape(rows, width), log_totals


def solution(mesh):
    in_specs = (
        P(("groups", "slab"), None),
        P(("groups", "slab"), None),
        P(("groups", "slab"), None),
        P("groups", None),
    )
    out_specs = (P(("groups", "slab"), None), P(("groups", "slab"), None))
    return jax.shard_map(shards, mesh=mesh, in_specs=in_specs, out_specs=out_specs, check_vma=False)
```

```python
import functools
import math

import jax
import jax.numpy as jnp
from jax import lax
from jax.experimental import pallas as pl
from jax.experimental.pallas import tpu as pltpu
from jax.sharding import PartitionSpec as P

HD = 128
BLOCK = 128
SUB = 8
TILE = 16
CHUNK = 8
MESH = pl.DeviceIdType.MESH

masked_score = -1e30


def kernel(
    n, q_hbm, k_hbm, v_hbm, ids_hbm, att_ref, log_ref,
    q_raw, ids, kbuf, vbuf, held, bias, give, pre, out, got,
    load_sem, q_send, q_recv, f_send, f_recv, p_send, p_recv, o_send, o_recv,
):
    me = lax.axis_index("slab")
    half = n // 2
    core = lax.rem(me, 2)
    other = 1 - core
    spot = me // 2
    sibling = me + 1 - 2 * core
    heads = held.shape[2]
    kv_heads = kbuf.shape[1] // HD
    pairs = heads // TILE
    span = kbuf.shape[0]
    blocks_here = span // BLOCK
    chunk = min(CHUNK, half)
    chunks = half // chunk
    factor = 1.0 / math.sqrt(HD)
    factor2 = factor * math.log2(math.e)

    barrier = pltpu.get_barrier_semaphore()

    @pl.loop(1, n)
    def _(i):
        peer = lax.rem(me + i, n)
        pl.semaphore_signal(barrier, inc=1, device_id={"slab": peer}, device_id_type=MESH)

    loads = [
        pltpu.make_async_copy(src, dst, load_sem.at[at])
        for at, (src, dst) in enumerate(((q_hbm, q_raw), (ids_hbm, ids), (k_hbm, kbuf), (v_hbm, vbuf)))
    ]
    for load in loads:
        load.start()

    loads[0].wait()
    row = q_raw[...].astype(jnp.float32)
    held[core, spot] = jnp.concatenate(
        [row[:, h * HD : (h + 1) * HD] for h in range(heads)], axis=0
    ).astype(jnp.bfloat16)

    def remote(src, dst, send, recv, peer):
        return pltpu.make_async_remote_copy(
            src_ref=src, dst_ref=dst, send_sem=send, recv_sem=recv,
            device_id={"slab": peer}, device_id_type=MESH,
        )

    def spot_at(i):
        return lax.rem(spot + i, half)

    pl.semaphore_wait(barrier, n - 1)

    @pl.loop(1, half)
    def _(i):
        own = held.at[core, spot]
        remote(own, own, q_send, q_recv.at[spot], spot_at(i) * 2 + core).start()

    def forward(at):
        remote(held.at[core, at], held.at[core, at], f_send, f_recv, sibling).start()

    forward(spot)

    loads[1].wait()

    def each_chunk(body):
        if chunks == 1:
            body(0)
        else:
            pl.loop(0, chunks)(body)

    def fill_bias(c):
        rows = pl.ds(c * chunk, chunk)
        both = ids[pl.ds(c * 2 * chunk, 2 * chunk)]
        wide = jnp.broadcast_to(both[:, None, :], (2 * chunk, SUB, ids.shape[1]))
        for j in range(blocks_here):
            hit = jnp.where(wide == me * blocks_here + j, 0.0, masked_score)
            hit = jnp.broadcast_to(jnp.max(hit, axis=-1, keepdims=True), (2 * chunk, SUB, BLOCK))
            hit = hit.reshape(chunk, 2, SUB, BLOCK)
            for side in range(2):
                bias[side, rows, :, j * BLOCK : (j + 1) * BLOCK] = hit[:, side]

    each_chunk(fill_bias)

    @pl.loop(1, half)
    def _(i):
        at = spot_at(half - i)
        remote(held.at[core, at], held.at[core, at], q_send, q_recv.at[at], sibling).wait_recv()
        forward(at)

    loads[2].wait()
    loads[3].wait()

    lane = lax.broadcasted_iota(jnp.int32, (chunk, SUB, HD), 2)
    sub = lax.broadcasted_iota(jnp.int32, (chunk * TILE, HD), 0)
    first = (lax.rem(sub, TILE) < SUB).astype(jnp.float32).astype(jnp.bfloat16)
    second = (lax.rem(sub, TILE) >= SUB).astype(jnp.float32).astype(jnp.bfloat16)

    def partial(side, rows, p):
        rows16 = slice(TILE * p, TILE * (p + 1))
        cols = slice(2 * HD * p, 2 * HD * (p + 1))
        q = held[side, rows, rows16, :].reshape(chunk * TILE, HD)
        q = jnp.concatenate([q * first, q * second], axis=1)
        scores = lax.dot_general(
            q, kbuf[:, cols], (((1,), (1,)), ((), ())), preferred_element_type=jnp.float32
        ).reshape(chunk, 2, SUB, span)
        scores = scores + bias[side, rows][:, None]
        peak = jnp.max(scores, axis=-1, keepdims=True)
        weights = jnp.exp2((scores - peak) * factor2)
        total = jnp.sum(weights, axis=-1, keepdims=True)
        mixed = jnp.dot(
            weights.astype(jnp.bfloat16).reshape(chunk * TILE, span), vbuf[:, cols],
            preferred_element_type=jnp.float32,
        ).reshape(chunk, 2, SUB, 2 * HD)
        mixed = [mixed[:, 0, :, :HD] / total[:, 0], mixed[:, 1, :, HD:] / total[:, 1]]
        logs = peak * factor + jnp.log(total)
        return mixed, [logs[:, 0], logs[:, 1]]

    def put(ref, rows, p, mixed):
        mixed = jnp.concatenate([part[:, None] for part in mixed], axis=1)
        ref[rows, TILE * p : TILE * (p + 1), :] = mixed.reshape(chunk, TILE, HD).astype(jnp.bfloat16)

    def put_logs(ref, rows, columns):
        logs = jnp.zeros((chunk, SUB, HD), jnp.float32)
        for k, column in enumerate(columns):
            logs = jnp.where(lax.rem(lane, kv_heads) == k, column, logs)
        high = logs.astype(jnp.bfloat16).astype(jnp.float32)
        rest = logs - high
        middle = rest.astype(jnp.bfloat16).astype(jnp.float32)
        low = rest - middle
        logs = jnp.where(lane < kv_heads, high, jnp.where(lane < 2 * kv_heads, middle, low))
        logs = jnp.where(lane < 3 * kv_heads, logs, 0.0)
        logs = jnp.concatenate([logs, jnp.zeros_like(logs)], axis=1)
        ref[rows, heads : heads + TILE, :] = logs.astype(jnp.bfloat16)

    def take_logs(ref, rows):
        logs = ref[rows, heads : heads + TILE, :].astype(jnp.float32)[:, :SUB]
        return (
            logs[..., :kv_heads] + logs[..., kv_heads : 2 * kv_heads] + logs[..., 2 * kv_heads : 3 * kv_heads]
        )

    def for_sibling(c):
        rows = pl.ds(c * chunk, chunk)
        columns = []
        for p in range(pairs):
            mixed, logs = partial(core, rows, p)
            put(give, rows, p, mixed)
            columns += logs
        put_logs(give, rows, columns)

    each_chunk(for_sibling)
    to_sibling = remote(give, pre, p_send, p_recv, sibling)
    to_sibling.start()

    whole_side = held.at[other]
    remote(whole_side, whole_side, f_send, f_recv, sibling).wait_recv()
    to_sibling.wait_recv()

    def for_owners(c):
        rows = pl.ds(c * chunk, chunk)
        found = [partial(other, rows, p) for p in range(pairs)]
        theirs = take_logs(pre, rows)
        columns = []
        for p in range(pairs):
            mixed, logs = found[p]
            parts = pre[rows, TILE * p : TILE * (p + 1), :].astype(jnp.float32).reshape(chunk, 2, SUB, HD)
            joined = []
            for at in range(2):
                mine, their = logs[at], theirs[:, :, 2 * p + at : 2 * p + at + 1]
                peak = jnp.maximum(mine, their)
                mine, their = jnp.exp(mine - peak), jnp.exp(their - peak)
                total = mine + their
                joined.append((mixed[at] * mine + parts[:, at] * their) / total)
                columns.append(peak + jnp.log(total))
            put(out, rows, p, joined)
        put_logs(out, rows, columns)

    each_chunk(for_owners)

    @pl.loop(1, half + 1)
    def _(i):
        at = spot_at(i)
        remote(out.at[at], got.at[spot], o_send, o_recv, at * 2 + other).start()

    remote(out, got, o_send, o_recv, sibling).wait_recv()
    logs = take_logs(got, slice(None))
    peak = jnp.max(logs, axis=0)
    shares = jnp.exp(logs - peak[None])
    total = jnp.sum(shares, axis=0)
    shares = shares / total[None]
    joint = peak + jnp.log(total)

    head_lane = lax.broadcasted_iota(jnp.int32, (SUB, heads), 1)
    head_sub = lax.broadcasted_iota(jnp.int32, (SUB, heads), 0)
    spread = jnp.zeros((SUB, heads), jnp.float32)
    for k in range(kv_heads):
        spread = jnp.where(head_lane // SUB == k, joint[:, k : k + 1], spread)
    spread = jnp.where(lax.rem(head_lane, SUB) == head_sub, spread, 0.0)
    log_ref[...] = jnp.sum(spread, axis=0, keepdims=True)

    for p in range(pairs):
        rows16 = slice(TILE * p, TILE * (p + 1))
        parts = got[:, rows16, :].astype(jnp.float32).reshape(half, 2, SUB, HD)
        merged = [
            jnp.sum(parts[:, at] * shares[:, :, 2 * p + at : 2 * p + at + 1], axis=0) for at in range(2)
        ]
        att_ref[rows16, :] = jnp.concatenate(merged, axis=0).astype(jnp.bfloat16)

    sent = held.at[core, pl.ds(0, half - 1)]
    remote(sent, sent, q_send, f_recv, sibling).wait_send()
    remote(whole_side, whole_side, f_send, f_recv, sibling).wait_send()
    to_sibling.wait_send()
    remote(out, got, o_send, o_recv, sibling).wait_send()


def shards(queries, prefix_keys, prefix_values, block_ids):
    n = lax.axis_size("slab")
    rows, width = queries.shape
    span, kv_width = prefix_keys.shape
    heads = width // HD
    half = n // 2
    assert rows == 1 and block_ids.shape[0] == n and heads == SUB * (kv_width // HD) and n % 2 == 0
    anywhere = pl.BlockSpec(memory_space=pltpu.HBM)
    in_vmem = pl.BlockSpec(memory_space=pltpu.VMEM)
    attended, log_totals = pl.pallas_call(
        functools.partial(kernel, n),
        out_shape=(
            pltpu.VMEM((heads, HD), jnp.bfloat16),
            pltpu.VMEM((1, heads), jnp.float32),
        ),
        in_specs=[anywhere] * 4,
        out_specs=(in_vmem, in_vmem),
        scratch_shapes=[
            pltpu.VMEM((1, width), jnp.bfloat16),
            pltpu.VMEM(block_ids.shape, jnp.int32),
            pltpu.VMEM((span, kv_width), jnp.bfloat16),
            pltpu.VMEM((span, kv_width), jnp.bfloat16),
            pltpu.VMEM((2, half, heads, HD), jnp.bfloat16),
            pltpu.VMEM((2, half, SUB, span), jnp.float32),
            pltpu.VMEM((half, heads + TILE, HD), jnp.bfloat16),
            pltpu.VMEM((half, heads + TILE, HD), jnp.bfloat16),
            pltpu.VMEM((half, heads + TILE, HD), jnp.bfloat16),
            pltpu.VMEM((half, heads + TILE, HD), jnp.bfloat16),
            pltpu.SemaphoreType.DMA((4,)),
            pltpu.SemaphoreType.DMA,
            pltpu.SemaphoreType.DMA((half,)),
        ] + [pltpu.SemaphoreType.DMA] * 6,
        compiler_params=pltpu.CompilerParams(
            collective_id=0, has_side_effects=True, vmem_limit_bytes=60 * 1024 * 1024
        ),
        cost_estimate=pl.CostEstimate(
            flops=8 * n * heads * span * HD,
            bytes_accessed=4 * span * kv_width,
            transcendentals=n * heads * span,
        ),
    )(queries, prefix_keys, prefix_values, block_ids)
    return attended.reshape(rows, width), log_totals


def solution(mesh):
    in_specs = (
        P(("groups", "slab"), None),
        P(("groups", "slab"), None),
        P(("groups", "slab"), None),
        P("groups", None),
    )
    out_specs = (P(("groups", "slab"), None), P(("groups", "slab"), None))
    return jax.shard_map(shards, mesh=mesh, in_specs=in_specs, out_specs=out_specs, check_vma=False)
```
